256 devices in a mesh: dp: 32 (over y_hi, z, core), blk: 8 (over y_lo, x).
Axes of the slice: x: 4, y: 4 (y_hi: 2, y_lo: 2; y = y_hi * 2 + y_lo), z: 8, core: 2. Of those that a mesh axis runs over, the one named last changes fastest.
Arguments:
- tokens: bfloat16 [65536, 2048], P(('dp', 'blk')), may hold values from -24 to 24
- cotangent: bfloat16 [65536, 2048], P(('dp', 'blk')), may hold values from -48 to 48
- slot_token: int32 [57344], P(('dp', 'blk')), may hold values from 0 to 256, as said below
- slot_gate: bfloat16 [57344], P(('dp', 'blk')), may hold values from 0.049804688 to 0.5
- w_gate: bfloat16 [768, 2048], P('blk'), may hold values from -0.125 to 0.125
- w_up: bfloat16 [768, 2048], P('blk'), may hold values from -0.125 to 0.125
- w_down: bfloat16 [768, 2048], P('blk'), may hold values from -0.21875 to 0.21875
Outputs:
- token_grad: bfloat16 [65536, 2048], P(('dp', 'blk'))
- gate_grad: float32 [57344], P(('dp', 'blk'))
- grad_gate: bfloat16 [768, 2048], P('blk', 'dp')
- grad_up: bfloat16 [768, 2048], P('blk', 'dp')
- grad_down: bfloat16 [768, 2048], P('blk', 'dp')
The draws below stay inside these ranges and needn't reach their ends.
Inputs may be any that keep to these rules, and one draw needn't show every extreme that they name: `slot_token`: on each device its 224 slots name distinct tokens of that same device; the value 256 marks an empty slot, and every device has at least one empty slot.
All inputs are finite; a program needn't handle non-finite values.
Results may differ from the reference program's by a relative error of at most 0.018.
Values may be sent and summed in bfloat16 or wider, within the bound.
A program may use at most 128 MiB of HBM per device.

```python
import math
import jax
import jax.numpy as jnp
from jax import lax

D = 2048
H = 768
TOK_DEV = 256
CAP = 224
TOKENS = 65536
SLOTS = 57344


def draw_slot_token(key, part):
    key = jax.random.fold_in(key, 7)
    count = SLOTS // CAP
    keys = jax.random.split(key, count)

    def one_device(sub):
        first, second, third = jax.random.split(sub, 3)
        chosen = jax.random.permutation(first, TOK_DEV)[:CAP]
        empty = jax.random.randint(second, (CAP,), 0, 4) == 0
        forced = jnp.arange(CAP) == jax.random.randint(third, (), 0, CAP)
        return jnp.where(empty | forced, TOK_DEV, chosen).astype(jnp.int32)
    return jax.vmap(one_device)(keys).reshape(SLOTS)


def with_spikes(array, own_key, source, target, shards_of, factor):
    def block_of(position):
        return (jnp.arange(array.shape[position]) // (array.shape[position] // shards_of)).reshape((-1,) + (1,) * (array.ndim - 1 - position))

    first = jax.random.permutation(own_key, shards_of)[block_of(target)]
    second = (block_of(target) + shards_of // 2) % shards_of
    return jnp.where((block_of(source) == first) | (block_of(source) == second), factor * array, array)


def block_levels(key, shape, pieces, low, largest):
    factor_of = 1.0
    for axis_at, shards_of in pieces:
        steps = jax.random.uniform(jax.random.fold_in(jax.random.fold_in(key, 6), axis_at), (shards_of,), jnp.float32, low / len(pieces), largest / len(pieces))
        factor_of = factor_of * jnp.repeat(jnp.exp(steps), shape[axis_at] // shards_of).reshape((-1,) + (1,) * (len(shape) - 1 - axis_at))
    return factor_of


def bell_draw(stream_key, shape, scale, bound, pieces=(), dtype=jnp.bfloat16):
    gain = block_levels(stream_key, shape, pieces, -0.22, 0.18) if pieces else 1.0
    drawn = jax.random.normal(stream_key, shape, jnp.float32) * scale * gain
    return jnp.minimum(jnp.maximum(drawn, -bound), bound).astype(dtype)


def bell_draw_with(rng, shape, deviation, most, cuts, heavy, held_as=jnp.bfloat16):
    values = deviation * jax.random.normal(rng, shape, jnp.float32)
    if cuts:
        values = values * block_levels(rng, shape, cuts, -0.22, 0.18)
    return jnp.clip(with_spikes(values, jax.random.fold_in(rng, 3), *heavy), -most, most).astype(held_as)


def setup_inputs(seed: int = 0) -> dict:
    streams_of = jax.random.split(jax.random.key(seed), 8)
    tokens = bell_draw_with(streams_of[0], (TOKENS, D), 1.0, 24.0, ((0, 256),), (0, 1, 256, 6.0))
    cotangent = bell_draw_with(streams_of[1], (TOKENS, D), 2.0, 48.0, ((0, 256),), (0, 1, 256, 6.0))
    slot_token = draw_slot_token(jax.random.fold_in(streams_of[7], 71), 0)
    slot_gate = jnp.clip(jnp.exp(math.log(0.5) - 2.306499 * jax.random.uniform(streams_of[3], (SLOTS,), jnp.float32) ** block_levels(streams_of[3], (SLOTS,), ((0, 256),), -0.2, 0.2)), 0.049804688, 0.5).astype(jnp.bfloat16)
    w_gate = bell_draw(streams_of[4], (H, D), D ** -0.5, 0.125, ((0, 8),))
    w_up = bell_draw(streams_of[5], (H, D), D ** -0.5, 0.125, ((0, 8),))
    w_down = bell_draw(streams_of[6], (H, D), H ** -0.5, 0.21875, ((0, 8),))
    return dict(tokens=tokens, cotangent=cotangent, slot_token=slot_token, slot_gate=slot_gate, w_gate=w_gate, w_up=w_up, w_down=w_down)


def row_dot(left, right):
    return lax.dot_general(left, right, (((1,), (1,)), ((), ())), preferred_element_type=jnp.float32)


def col_dot(left, right):
    return lax.dot_general(left, right, (((0,), (0,)), ((), ())), preferred_element_type=jnp.float32)


def device_terms(x_dev, dy_dev, index, gate, w_gate, w_up, w_down):
    zero_row = jnp.zeros((1, D), jnp.bfloat16)
    slot_x = jnp.take(jnp.concatenate([x_dev, zero_row], axis=0), index, axis=0)
    slot_dy = jnp.take(jnp.concatenate([dy_dev, zero_row], axis=0), index, axis=0)
    weight = gate.astype(jnp.float32)[:, None]
    g = row_dot(slot_x, w_gate)
    u = row_dot(slot_x, w_up)
    sig = jax.nn.sigmoid(g)
    act = g * sig
    hid = act * u
    stored = lax.optimization_barrier(hid.astype(jnp.bfloat16))
    raw = row_dot(slot_dy, w_down)
    gate_part = jnp.sum(stored.astype(jnp.float32) * raw, axis=1)
    grad_h = weight * raw
    grad_g = (grad_h * u * sig * (1.0 + g * (1.0 - sig))).astype(jnp.bfloat16)
    grad_u = (grad_h * act).astype(jnp.bfloat16)
    scaled = (weight * hid).astype(jnp.bfloat16)
    dx_slot = jnp.dot(grad_g, w_gate, preferred_element_type=jnp.float32) + jnp.dot(grad_u, w_up, preferred_element_type=jnp.float32)
    dx_tok = jnp.zeros((TOK_DEV + 1, D), jnp.float32).at[index].add(dx_slot)[:TOK_DEV].astype(jnp.bfloat16)
    grads = jnp.stack([col_dot(grad_g, slot_x), col_dot(grad_u, slot_x), col_dot(scaled, slot_dy)])
    return dx_tok, gate_part, grads


def reference(tokens, cotangent, slot_token, slot_gate, w_gate, w_up, w_down):
    count = TOKENS // TOK_DEV
    x_all = tokens.reshape(count, TOK_DEV, D)
    dy_all = cotangent.reshape(count, TOK_DEV, D)
    idx_all = slot_token.reshape(count, CAP).astype(jnp.int32)
    gate_all = slot_gate.reshape(count, CAP)

    def step(total, items):
        dx_tok, gate_part, grads = device_terms(items[0], items[1], items[2], items[3], w_gate, w_up, w_down)
        return total + grads, (dx_tok, gate_part)

    total, (dx_tok, gate_part) = lax.scan(step, jnp.zeros((3, H, D), jnp.float32), (x_all, dy_all, idx_all, gate_all))
    scaled = total * (TOKENS ** -0.5)
    return (dx_tok.reshape(TOKENS, D), gate_part.reshape(SLOTS), scaled[0].astype(jnp.bfloat16), scaled[1].astype(jnp.bfloat16), scaled[2].astype(jnp.bfloat16))
```

```python
import jax
import jax.numpy as jnp
from jax import lax
from jax.experimental import pallas as pl
from jax.experimental.pallas import tpu as pltpu
from jax.sharding import PartitionSpec as P

MESH = pl.DeviceIdType.MESH
F32 = jnp.float32
BF16 = jnp.bfloat16
TICKS = 4
UNIT = 48


def dot_nt(a, b):
    return lax.dot_general(a, b, (((1,), (1,)), ((), ())), preferred_element_type=F32)


def dot_nn(a, b):
    return lax.dot_general(a, b, (((1,), (0,)), ((), ())), preferred_element_type=F32)


def kernel(
    factor, tok, cot, slot, gate, wg, wu, wd,
    out_x, out_gate, out_g, out_u, out_d,
    xb, db, cb, ups, raws, wgu, wdn, dgs, grad, recv, fin, pack, a2, dxo, dxs, dxr, gs, gr,
    loc_sem, sib_s, sib_r, ax_s, ay_s, ag_r, zs, zr, ps, pr,
):
    dp, blk = lax.axis_index("dp"), lax.axis_index("blk")
    c, z, yh = dp % 2, (dp // 2) % 8, dp // 16
    x, yl = blk % 4, blk // 4
    y = yh * 2 + yl
    home = c == yl
    away = c != yl

    def device(xx, yy, zz, cc):
        return ((yy // 2) * 16 + zz * 2 + cc, (yy % 2) * 4 + xx)

    right, left = device((x + 1) % 4, y, z, c), device((x + 3) % 4, y, z, c)
    above, below = device(x, (y + 1) % 4, z, c), device(x, (y + 3) % 4, z, c)
    zside = (device(x, y, (z + 1) % 8, c), device(x, y, (z + 7) % 8, c))
    sibling = device(x, y, z, 1 - c)
    place = y * 4 + x

    loads = [
        pltpu.make_async_copy(tok, xb.at[pl.ds(0, 256)], loc_sem.at[0]),
        pltpu.make_async_copy(cot, db.at[pl.ds(0, 256)], loc_sem.at[1]),
    ]
    wloads = [
        pltpu.make_async_copy(wg.at[pl.ds(0, 48)], wgu.at[pl.ds(0, 48)], loc_sem.at[2]),
        pltpu.make_async_copy(wu.at[pl.ds(0, 48)], wgu.at[pl.ds(48, 48)], loc_sem.at[3]),
        pltpu.make_async_copy(wg.at[pl.ds(48, 48)], wgu.at[pl.ds(96, 48)], loc_sem.at[4]),
        pltpu.make_async_copy(wu.at[pl.ds(48, 48)], wgu.at[pl.ds(144, 48)], loc_sem.at[5]),
        pltpu.make_async_copy(wd, wdn.at[pl.ds(0, 96)], loc_sem.at[6]),
    ]

    @pl.when(home)
    def _():
        for copy in wloads:
            copy.start()

    for copy in loads:
        copy.start()

    barrier = pltpu.get_barrier_semaphore()

    def greet(target):
        pl.semaphore_signal(barrier, inc=1, device_id=target, device_id_type=MESH)

    greet(zside[0])
    greet(zside[1])
    greet(sibling)

    def greet_plane(r, carry):
        other = (place + r) % 16
        greet(device(other % 4, other // 4, z, yl))
        return carry

    lax.fori_loop(1, 16, greet_plane, 0)

    @pl.when(away)
    def _():
        greet(above)
        greet(below)

    slots = jnp.broadcast_to(slot[...].astype(F32), (128, 224)).T[:, 0:1]
    gates = jnp.broadcast_to(gate[...].astype(F32), (128, 224)).T[:, 0:1]
    token_of = lax.broadcasted_iota(jnp.int32, (224, 256), 1).astype(F32)
    named = token_of == slots
    cb[0] = jnp.broadcast_to(
        jnp.sum(jnp.where(named, gates, 0.0), axis=0, keepdims=True), (8, 256)
    )

    @pl.when(home)
    def _():
        for copy in wloads:
            copy.wait()

    for copy in loads:
        copy.wait()
    pl.semaphore_wait(barrier, 19)

    def remote(src, dst, s_sem, r_sem, target):
        return pltpu.make_async_remote_copy(
            src_ref=src, dst_ref=dst, send_sem=s_sem, recv_sem=r_sem,
            device_id=target, device_id_type=MESH,
        )

    def unit(t, i):
        return (wgu.at[pl.ds(192 * t + 96 * i, 96)], wdn.at[pl.ds(96 * t + 48 * i, 48)])

    def send_unit(src, dst, sem, n, target):
        a, b = unit(*src), unit(*dst)
        return [
            remote(a[p], b[p], sem.at[n, p], ag_r.at[dst[0], dst[1], p], target)
            for p in range(2)
        ]

    def ring_a():
        return send_unit((0, 0), (1, 0), ax_s, 0, right) + send_unit((0, 0), (1, 1), ax_s, 1, left)

    def ring_b():
        return send_unit((0, 1), (2, 0), ax_s, 2, right) + send_unit((0, 1), (2, 1), ax_s, 3, left)

    def ring_f(t):
        if t == 1:
            return send_unit((1, 0), (3, 0), ax_s, 4, right)
        return send_unit((2, 1), (3, 1), ax_s, 5, left)

    def up_down(t):
        return send_unit((t, 0), (t, 0), ay_s, 2 * t, below) + send_unit((t, 1), (t, 1), ay_s, 2 * t + 1, above)

    def start(copies):
        for copy in copies:
            copy.start()

    def wait_unit(t, i):
        for p in range(2):
            ref = unit(t, i)[p]
            remote(ref, ref, ax_s.at[0, p], ag_r.at[t, i, p], sibling).wait_recv()

    sib = [
        remote(xb.at[pl.ds(0, 256)], xb.at[pl.ds(256, 256)], sib_s.at[0], sib_r.at[0], sibling),
        remote(db.at[pl.ds(0, 256)], db.at[pl.ds(256, 256)], sib_s.at[1], sib_r.at[1], sibling),
        remote(cb.at[0], cb.at[1], sib_s.at[2], sib_r.at[2], sibling),
    ]

    @pl.when(home)
    def _():
        start(ring_a() + up_down(0))

    start(sib)

    gate_acc = [jnp.zeros((1, 512), F32)]

    def compute(t):
        top, low = 192 * t, 96 * t

        def forward(n, carry):
            rows = pl.ds(pl.multiple_of(n * 256, 256), 256)
            ups[n] = dot_nt(wgu[pl.ds(top, 192)], xb[rows])
            return carry

        def outer(n, carry):
            rows = pl.ds(pl.multiple_of(n * 256, 256), 256)
            raws[n] = dot_nt(wdn[pl.ds(low, 96)], db[rows])
            return carry

        lax.fori_loop(0, 2, forward, 0)
        lax.fori_loop(0, 2, outer, 0)
        gu = jnp.concatenate([ups[0], ups[1]], axis=1)
        raw2 = jnp.concatenate([raws[0], raws[1]], axis=1)
        weight = jnp.concatenate([cb[0, 0:1], cb[1, 0:1]], axis=1)
        scaled = []
        for i in range(2):
            g = gu[96 * i : 96 * i + 48]
            u = gu[96 * i + 48 : 96 * i + 96]
            raw = raw2[48 * i : 48 * i + 48]
            sig = 1.0 / (1.0 + jnp.exp(-g))
            act = g * sig
            hid = act * u
            stored = hid.astype(BF16).astype(F32)
            gate_acc[0] = gate_acc[0] + jnp.sum(stored * raw, axis=0, keepdims=True)
            dh = weight * raw
            dgs[pl.ds(top + 96 * i, 48)] = (dh * u * sig * (1.0 + g * (1.0 - sig))).astype(BF16)
            dgs[pl.ds(top + 96 * i + 48, 48)] = (dh * act).astype(BF16)
            scaled.append((weight * hid).astype(BF16))
        q = jnp.concatenate(scaled, axis=0)
        dgu = dgs[pl.ds(top, 192)]

        def columns(n, carry):
            cols = pl.ds(pl.multiple_of(n * 256, 256), 256)
            part = dot_nn(dgu, xb[:, cols]).astype(BF16)
            for k in range(2):
                grad[t, 2 * (n % 4) + k, n // 4, 0:192] = part[:, 128 * k : 128 * k + 128]
            return carry

        def columns_down(n, carry):
            cols = pl.ds(pl.multiple_of(n * 256, 256), 256)
            down = dot_nn(q, db[:, cols]).astype(BF16)
            for k in range(2):
                grad[t, 2 * (n % 4) + k, n // 4, 192:288] = down[:, 128 * k : 128 * k + 128]
            return carry

        lax.fori_loop(0, 8, columns_down, 0)
        lax.fori_loop(0, 8, columns, 0)

    def ring(t, way, step):
        sign = 1 if way == 0 else 7
        dest = (z + sign * (5 - step)) % 8
        if step == 1:
            src, dst = grad.at[t, dest, way], recv.at[t, way, 0, way]
        else:
            src, dst = grad.at[t, dest], recv.at[t, way, step - 1]
        return remote(src, dst, zs.at[t, way, step - 1], zr.at[t, way, step - 1], zside[way])

    def first(t):
        for way in range(2):
            ring(t, way, 1).start()

    def pass_on(t, step):
        for way in range(2):
            ring(t, way, step - 1).wait_recv()
            sign = 1 if way == 0 else 7
            dest = (z + sign * (5 - step)) % 8
            for h in (way,) if step == 2 else (0, 1):
                total = grad[t, dest, h].astype(F32) + recv[t, way, step - 2, h].astype(F32)
                grad[t, dest, h] = total.astype(BF16)
            ring(t, way, step).start()

    def finish(t):
        for way in range(2):
            ring(t, way, 4).wait_recv()
        for h in range(2):
            fin[t, h] = (
                grad[t, z, h].astype(F32) + recv[t, 0, 3, h].astype(F32) + recv[t, 1, 3, h].astype(F32)
            )

    low_lanes = lax.broadcasted_iota(jnp.int32, (144, 128), 1) < 64
    halves = (((0, 0), (0, 1)), ((1, 0), (2, 0)), ((1, 1), (2, 1)), ((3, 0), (3, 1)))
    offset = (0, 3, 1, 2)

    def rows_of(t, i, h):
        return jnp.concatenate(
            [fin[t, h, pl.ds(96 * i, 96)], fin[t, h, pl.ds(192 + 48 * i, 48)]], axis=0
        )

    def deliver_copy(j, yy, kk):
        h, k = (yh + yy) % 2, (c + kk) % 2
        target = device((x + offset[j]) % 4, 2 * h + c, z, k)
        return remote(pack.at[j, h, k], a2.at[place], ps.at[j, yy, kk], pr.at[place], target)

    def deliver(j):
        for h in range(2):
            a, b = rows_of(*halves[j][0], h), rows_of(*halves[j][1], h)
            pack[j, h, 0] = jnp.where(low_lanes, a, pltpu.roll(b, 64, 1)).astype(BF16)
            pack[j, h, 1] = jnp.where(low_lanes, pltpu.roll(a, 64, 1), b).astype(BF16)
        for yy in range(2):
            for kk in range(2):
                if (j, yy, kk) == (0, 0, 0):

                    @pl.when(away)
                    def _():
                        deliver_copy(0, 0, 0).start()

                    @pl.when(home)
                    def _():
                        a2[place] = pack[0, yh, c]

                else:
                    deliver_copy(j, yy, kk).start()

    dx_copy = remote(dxs, dxr, sib_s.at[3], sib_r.at[3], sibling)
    gate_copy = remote(gs, gr, sib_s.at[4], sib_r.at[4], sibling)

    def token_part():
        gs[...] = jnp.broadcast_to(gate_acc[0][:, 256:], (8, 256))
        gate_copy.start()
        left_side = dgs[...].T

        def columns(n, carry):
            cols = pl.ds(pl.multiple_of(n * 256, 256), 256)
            part = dot_nn(left_side, wgu[:, cols])
            dxo[:, cols] = part[:256]
            dxs[:, cols] = part[256:]
            return carry

        lax.fori_loop(0, 8, columns, 0)
        dx_copy.start()

    def weights_of(t):
        @pl.when(away)
        def _():
            wait_unit(t, 0)
            wait_unit(t, 1)

        if t > 0:

            @pl.when(home)
            def _():
                wait_unit(t, 0)
                wait_unit(t, 1)
                if t < 3:
                    start(ring_f(t))
                start(up_down(t))

    for copy in sib:
        copy.wait_recv()
    weights_of(0)
    compute(0)
    first(0)

    @pl.when(home)
    def _():
        start(ring_b())

    pass_on(0, 2)
    weights_of(1)
    compute(1)
    first(1)
    pass_on(0, 3)
    pass_on(1, 2)
    pass_on(0, 4)
    weights_of(2)
    compute(2)
    first(2)
    finish(0)
    deliver(0)
    pass_on(1, 3)
    pass_on(2, 2)
    pass_on(1, 4)
    weights_of(3)
    compute(3)
    first(3)
    finish(1)
    pass_on(2, 3)
    pass_on(3, 2)
    token_part()
    pass_on(2, 4)
    pass_on(3, 3)
    finish(2)
    deliver(1)
    deliver(2)
    pass_on(3, 4)

    gate_copy.wait_recv()
    gate_tok = gate_acc[0][:, :256] + gr[0:1]
    column = jnp.sum(jnp.where(named, gate_tok, 0.0), axis=1, keepdims=True)
    out_gate[...] = jnp.broadcast_to(column, (224, 128)).T[0:1]
    dx_copy.wait_recv()
    out_x[...] = (dxo[...] + dxr[...]).astype(BF16)

    finish(3)
    deliver(3)

    @pl.when(away)
    def _():
        remote(a2.at[place], a2.at[place], ps.at[0, 0, 0], pr.at[place], sibling).wait_recv()

    def arrival(r, carry):
        other = (place + r) % 16
        remote(a2.at[other], a2.at[other], ps.at[0, 0, 0], pr.at[other], sibling).wait_recv()
        return carry

    lax.fori_loop(1, 16, arrival, 0)
    total = a2[0].astype(F32)
    for s in range(1, 16):
        total = total + a2[s].astype(F32)
    total = total * factor
    first_half, second_half = total[:, :64], pltpu.roll(total, 64, 1)[:, :64]
    for m, out in enumerate((out_g, out_u, out_d)):
        out[0:48] = first_half[48 * m : 48 * m + 48].astype(BF16)
        out[48:96] = second_half[48 * m : 48 * m + 48].astype(BF16)

    for copy in sib + [dx_copy, gate_copy]:
        copy.wait_send()
    for t in range(TICKS):
        for way in range(2):
            for step in range(1, 5):
                ring(t, way, step).wait_send()
    for j in range(4):
        for yy in range(2):
            for kk in range(2):
                if (j, yy, kk) == (0, 0, 0):

                    @pl.when(away)
                    def _():
                        deliver_copy(0, 0, 0).wait_send()

                else:
                    deliver_copy(j, yy, kk).wait_send()

    @pl.when(home)
    def _():
        for copy in ring_a() + ring_b() + ring_f(1) + ring_f(2):
            copy.wait_send()
        for t in range(TICKS):
            for copy in up_down(t):
                copy.wait_send()


def per_device(tokens, cotangent, slot_token, slot_gate, w_gate, w_up, w_down):
    factor = float(65536) ** (-0.5)
    vmem = pl.BlockSpec(memory_space=pltpu.VMEM)
    hbm = pl.BlockSpec(memory_space=pl.ANY)
    dma = pltpu.SemaphoreType.DMA
    outs = pl.pallas_call(
        lambda *refs: kernel(factor, *refs),
        out_shape=(
            jax.ShapeDtypeStruct((256, 2048), BF16),
            jax.ShapeDtypeStruct((1, 224), F32),
            jax.ShapeDtypeStruct((96, 64), BF16),
            jax.ShapeDtypeStruct((96, 64), BF16),
            jax.ShapeDtypeStruct((96, 64), BF16),
        ),
        in_specs=[hbm, hbm, vmem, vmem, hbm, hbm, hbm],
        out_specs=(vmem,) * 5,
        scratch_shapes=[
            pltpu.VMEM((512, 2048), BF16),
            pltpu.VMEM((512, 2048), BF16),
            pltpu.VMEM((2, 8, 256), F32),
            pltpu.VMEM((2, 192, 256), F32),
            pltpu.VMEM((2, 96, 256), F32),
            pltpu.VMEM((768, 2048), BF16),
            pltpu.VMEM((384, 2048), BF16),
            pltpu.VMEM((768, 512), BF16),
            pltpu.VMEM((4, 8, 2, 288, 128), BF16),
            pltpu.VMEM((4, 2, 4, 2, 288, 128), BF16),
            pltpu.VMEM((4, 2, 288, 128), F32),
            pltpu.VMEM((4, 2, 2, 144, 128), BF16),
            pltpu.VMEM((16, 144, 128), BF16),
            pltpu.VMEM((256, 2048), F32),
            pltpu.VMEM((256, 2048), F32),
            pltpu.VMEM((256, 2048), F32),
            pltpu.VMEM((8, 256), F32),
            pltpu.VMEM((8, 256), F32),
            dma((7,)),
            dma((5,)),
            dma((5,)),
            dma((6, 2)),
            dma((8, 2)),
            dma((4, 2, 2)),
            dma((4, 2, 4)),
            dma((4, 2, 4)),
            dma((4, 2, 2)),
            dma((16,)),
        ],
        compiler_params=pltpu.CompilerParams(
            collective_id=0, has_side_effects=True, vmem_limit_bytes=56 << 20
        ),
        name="expert_backward",
    )(tokens, cotangent, slot_token.reshape(1, 224), slot_gate.reshape(1, 224), w_gate, w_up, w_down)
    return (outs[0], outs[1].reshape(224), outs[2], outs[3], outs[4])


def solution(mesh):
    both = P(("dp", "blk"), None)
    flat = P(("dp", "blk"))
    rows = P("blk", None)
    block = P("blk", "dp")
    return jax.shard_map(
        per_device,
        mesh=mesh,
        in_specs=(both, both, flat, flat, rows, rows, rows),
        out_specs=(both, flat, block, block, block),
        check_vma=False,
    )
```

```python
import jax
import jax.numpy as jnp
from jax import lax
from jax.experimental import pallas as pl
from jax.experimental.pallas import tpu as pltpu
from jax.sharding import PartitionSpec as P

MESH = pl.DeviceIdType.MESH
F32 = jnp.float32
BF16 = jnp.bfloat16
TICKS = 4

RINGS = (
    (0, ((0, 0),)),
    (1, ((0, 1),)),
    (2, ((0, 0),)),
    (3, ((0, 0),)),
    (0, ((1, 1),)),
    (3, ((1, 1),)),
)


def dot_nt(a, b):
    return lax.dot_general(a, b, (((1,), (1,)), ((), ())), preferred_element_type=F32)


def dot_nn(a, b):
    return lax.dot_general(a, b, (((1,), (0,)), ((), ())), preferred_element_type=F32)


def kernel(
    factor, tok, cot, slot, gate, wg, wu, wd,
    out_x, out_gate, out_g, out_u, out_d,
    xb, db, xt, dt, cb, ups, raws, wgu, wdn, dgs, qs, grad, recv, fin, side, pack, a2, acc, dxo, dxs, dxr, gs, gr,
    loc_sem, sib_s, sib_r, ax_s, ay_s, ag_r, zs, zr, xs_, xr, ps, pr,
):
    dp, blk = lax.axis_index("dp"), lax.axis_index("blk")
    c, z, yh = dp % 2, (dp // 2) % 8, dp // 16
    x, yl = blk % 4, blk // 4
    y = yh * 2 + yl
    home = c == yl
    away = c != yl

    def device(xx, yy, zz, cc):
        return ((yy // 2) * 16 + zz * 2 + cc, (yy % 2) * 4 + xx)

    right, left = device((x + 1) % 4, y, z, c), device((x + 3) % 4, y, z, c)
    above, below = device(x, (y + 1) % 4, z, c), device(x, (y + 3) % 4, z, c)
    zside = (device(x, y, (z + 1) % 8, c), device(x, y, (z + 7) % 8, c))
    sibling = device(x, y, z, 1 - c)
    place = y * 4 + x

    loads = [
        pltpu.make_async_copy(tok, xb.at[pl.ds(0, 256)], loc_sem.at[0]),
        pltpu.make_async_copy(cot, db.at[pl.ds(0, 256)], loc_sem.at[1]),
    ]
    wloads = [
        pltpu.make_async_copy(wg.at[pl.ds(0, 48)], wgu.at[pl.ds(0, 48)], loc_sem.at[2]),
        pltpu.make_async_copy(wu.at[pl.ds(0, 48)], wgu.at[pl.ds(48, 48)], loc_sem.at[3]),
        pltpu.make_async_copy(wg.at[pl.ds(48, 48)], wgu.at[pl.ds(96, 48)], loc_sem.at[4]),
        pltpu.make_async_copy(wu.at[pl.ds(48, 48)], wgu.at[pl.ds(144, 48)], loc_sem.at[5]),
        pltpu.make_async_copy(wd, wdn.at[pl.ds(0, 96)], loc_sem.at[6]),
    ]

    @pl.when(home)
    def _():
        for copy in wloads:
            copy.start()

    for copy in loads:
        copy.start()

    barrier = pltpu.get_barrier_semaphore()

    def greet(target):
        pl.semaphore_signal(barrier, inc=1, device_id=target, device_id_type=MESH)

    greet(zside[0])
    greet(zside[1])
    greet(sibling)

    def greet_plane(r, carry):
        other = (place + r) % 16
        greet(device(other % 4, other // 4, z, yl))
        return carry

    lax.fori_loop(1, 16, greet_plane, 0)

    @pl.when(away)
    def _():
        greet(above)
        greet(below)
        greet(right)
        greet(left)

    slots = jnp.broadcast_to(slot[...].astype(F32), (128, 224)).T[:, 0:1]
    gates = jnp.broadcast_to(gate[...].astype(F32).reshape(1, 224), (128, 224)).T[:, 0:1]
    token_of = lax.broadcasted_iota(jnp.int32, (224, 256), 1).astype(F32)
    named = token_of == slots
    cb[0] = jnp.broadcast_to(
        jnp.sum(jnp.where(named, gates, 0.0), axis=0, keepdims=True), (8, 256)
    )

    @pl.when(home)
    def _():
        for copy in wloads:
            copy.wait()

    for copy in loads:
        copy.wait()
    pl.semaphore_wait(barrier, jnp.where(home, 19, 21))

    def remote(src, dst, s_sem, r_sem, target):
        return pltpu.make_async_remote_copy(
            src_ref=src, dst_ref=dst, send_sem=s_sem, recv_sem=r_sem,
            device_id=target, device_id_type=MESH,
        )

    def unit(t, i):
        return (wgu.at[pl.ds(192 * t + 96 * i, 96)], wdn.at[pl.ds(96 * t + 48 * i, 48)])

    def send_unit(src, dst, sem, n, target):
        a, b = unit(*src), unit(*dst)
        return [
            remote(a[p], b[p], sem.at[n, p], ag_r.at[dst[0], dst[1], p], target)
            for p in range(2)
        ]

    def ring_a():
        return send_unit((0, 0), (1, 0), ax_s, 0, right) + send_unit((0, 1), (1, 1), ax_s, 1, left)

    def ring_b():
        return send_unit((0, 1), (2, 0), ax_s, 2, right) + send_unit((0, 0), (2, 1), ax_s, 3, left)

    def ring_f():
        return send_unit((1, 0), (3, 0), ax_s, 4, right) + send_unit((1, 1), (3, 1), ax_s, 5, left)

    def up_down(t):
        copies = send_unit((t, 0), (t, 0), ay_s, 2 * t, below) + send_unit((t, 1), (t, 1), ay_s, 2 * t + 1, above)
        return copies if t < 3 else copies[1::2]

    def away_f():
        return ring_f()[0::2]

    def start(copies):
        for copy in copies:
            copy.start()

    def wait_unit(t, i):
        for p in range(2):
            ref = unit(t, i)[p]
            remote(ref, ref, ax_s.at[0, p], ag_r.at[t, i, p], sibling).wait_recv()

    sib = [
        remote(xb.at[pl.ds(0, 256)], xb.at[pl.ds(256, 256)], sib_s.at[0], sib_r.at[0], sibling),
        remote(db.at[pl.ds(0, 256)], db.at[pl.ds(256, 256)], sib_s.at[1], sib_r.at[1], sibling),
        remote(cb.at[0], cb.at[1], sib_s.at[2], sib_r.at[2], sibling),
    ]

    @pl.when(home)
    def _():
        start(ring_a() + up_down(0))

    start(sib)

    gate_acc = [jnp.zeros((1, 512), F32)]

    def forward_part(t):
        top, low = 192 * t, 96 * t

        ups[...] = dot_nn(wgu[pl.ds(top, 192)], xt[...])
        raws[...] = dot_nn(wdn[pl.ds(low, 96)], dt[...])
        gu = ups[...]
        raw2 = raws[...]
        weight = jnp.concatenate([cb[0, 0:1], cb[1, 0:1]], axis=1)
        scaled = []
        for i in range(2):
            g = gu[96 * i : 96 * i + 48]
            u = gu[96 * i + 48 : 96 * i + 96]
            raw = raw2[48 * i : 48 * i + 48]
            sig = 1.0 / (1.0 + jnp.exp(-g))
            act = g * sig
            hid = act * u
            stored = hid.astype(BF16).astype(F32)
            gate_acc[0] = gate_acc[0] + jnp.sum(stored * raw, axis=0, keepdims=True)
            dh = weight * raw
            dgs[pl.ds(top + 96 * i, 48)] = (dh * u * sig * (1.0 + g * (1.0 - sig))).astype(BF16)
            dgs[pl.ds(top + 96 * i + 48, 48)] = (dh * act).astype(BF16)
            scaled.append((weight * hid).astype(BF16))
        qs[...] = jnp.concatenate(scaled, axis=0)

    def grad_part(t):
        q = qs[...]
        dgu = dgs[pl.ds(192 * t, 192)]

        for n in range(8):
            cols = slice(256 * n, 256 * n + 256)
            part = dot_nn(dgu, xb[:, cols]).astype(BF16)
            for k in range(2):
                lanes = slice(128 * k, 128 * k + 128)
                place_at = grad.at[t, 2 * (n % 4) + k, n // 4]
                place_at[0:96] = part[0:96, lanes]
                place_at[144:240] = part[96:192, lanes]
        for n in range(8):
            cols = slice(256 * n, 256 * n + 256)
            down = dot_nn(q, db[:, cols]).astype(BF16)
            for k in range(2):
                lanes = slice(128 * k, 128 * k + 128)
                place_at = grad.at[t, 2 * (n % 4) + k, n // 4]
                place_at[96:144] = down[0:48, lanes]
                place_at[240:288] = down[48:96, lanes]

    def sends(ring, way, step):
        t, parts = ring
        return tuple(h for h, far in parts if step > 1 or far == way)

    def ring_copy(r, way, step):
        t = RINGS[r][0]
        half = sends(RINGS[r], way, step)
        sign = 1 if way == 0 else 7
        dest = (z + sign * (5 - step)) % 8
        if len(half) == 2:
            src, dst = grad.at[t, dest], recv.at[t, way, step - 1]
        else:
            src, dst = grad.at[t, dest, half[0]], recv.at[t, way, step - 1, half[0]]
        return remote(src, dst, zs.at[r, way, step - 1], zr.at[r, way, step - 1], zside[way])

    def stage_step(r, way, stage):
        return stage if sends(RINGS[r], way, 1) else stage + 1

    def first(r):
        for way in range(2):
            ring_copy(r, way, stage_step(r, way, 1)).start()

    def pass_on(r, stage):
        t = RINGS[r][0]
        for way in range(2):
            step = stage_step(r, way, stage)
            if step > 4:
                continue
            ring_copy(r, way, step - 1).wait_recv()
            sign = 1 if way == 0 else 7
            dest = (z + sign * (5 - step)) % 8
            for h in sends(RINGS[r], way, step - 1):
                total = grad[t, dest, h].astype(F32) + recv[t, way, step - 2, h].astype(F32)
                grad[t, dest, h] = total.astype(BF16)
            ring_copy(r, way, step).start()

    def finish(r):
        t, parts = RINGS[r]
        for way in range(2):
            ring_copy(r, way, 4).wait_recv()
        for h, _ in parts:
            fin[t, h] = (
                grad[t, z, h].astype(F32) + recv[t, 0, 3, h].astype(F32) + recv[t, 1, 3, h].astype(F32)
            )

    def side_copy(t, i):
        return remote(
            grad.at[t, :, 1, pl.ds(144 * i, 144)], side.at[t - 1, i],
            xs_.at[t - 1, i], xr.at[t - 1, i], left if i == 0 else right,
        )

    def side_send(t):
        for i in range(2):
            side_copy(t, i).start()

    def side_merge():
        for t in (1, 2):
            for i in range(2):
                side_copy(t, i).wait_recv()
        for i in range(2):
            rows = pl.ds(144 * i, 144)
            for k in range(8):
                total = grad[0, k, 1, rows].astype(F32) + side[0, i, k].astype(F32) + side[1, 1 - i, k].astype(F32)
                grad[0, k, 1, rows] = total.astype(BF16)

    low_lanes = lax.broadcasted_iota(jnp.int32, (144, 128), 1) < 64
    halves = (((0, 0), (0, 1)), ((1, 0), (2, 0)), ((2, 1), (1, 1)), ((3, 0), (3, 1)))
    offset = (0, 3, 1, 2)

    def rows_of(t, i, h):
        return fin[t, h, pl.ds(144 * i, 144)]

    def deliver_copy(j, h, kk):
        k = (c + kk) % 2
        target = device((x + offset[j]) % 4, 2 * h + c, z, k)
        return remote(pack.at[j, h, k], a2.at[place], ps.at[j, h, kk], pr.at[place], target)

    def deliver(j, h):
        a, b = rows_of(*halves[j][0], h), rows_of(*halves[j][1], h)
        pack[j, h, 0] = jnp.where(low_lanes, a, pltpu.roll(b, 64, 1)).astype(BF16)
        pack[j, h, 1] = jnp.where(low_lanes, pltpu.roll(a, 64, 1), b).astype(BF16)
        for kk in range(2):
            if (j, kk) == (0, 0):
                mine = jnp.logical_and(home, yh == h)

                @pl.when(mine)
                def _():
                    a2[place] = pack[0, h, c]

                @pl.when(jnp.logical_not(mine))
                def _():
                    deliver_copy(0, h, 0).start()

            else:
                deliver_copy(j, h, kk).start()

    dx_copy = remote(dxs, dxr, sib_s.at[3], sib_r.at[3], sibling)
    gate_copy = remote(gs, gr, sib_s.at[4], sib_r.at[4], sibling)

    def token_part():
        gs[...] = jnp.broadcast_to(gate_acc[0][:, 256:], (8, 256))
        gate_copy.start()
        left_side = dgs[...].T

        for n in range(8):
            cols = slice(256 * n, 256 * n + 256)
            part = dot_nn(left_side, wgu[:, cols])
            dxo[:, cols] = part[:256]
            dxs[:, cols] = part[256:]
        dx_copy.start()

    def weights_of(t):
        @pl.when(away)
        def _():
            wait_unit(t, 0)
            wait_unit(t, 1)
            if t == 1:
                start(away_f())

        if t > 0:

            @pl.when(home)
            def _():
                wait_unit(t, 0)
                wait_unit(t, 1)
                start((ring_f() if t == 1 else []) + up_down(t))

    xt[:, 0:256] = xb[0:256].T
    dt[:, 0:256] = db[0:256].T
    for copy in sib:
        copy.wait_recv()
    xt[:, 256:512] = xb[256:512].T
    dt[:, 256:512] = db[256:512].T
    weights_of(0)
    forward_part(0)

    @pl.when(home)
    def _():
        start(ring_b())

    grad_part(0)
    first(0)
    pass_on(0, 2)
    weights_of(1)
    forward_part(1)
    grad_part(1)
    first(1)

    @pl.when(away)
    def _():
        side_send(1)

    pass_on(0, 3)
    pass_on(1, 2)
    pass_on(0, 4)
    weights_of(2)
    forward_part(2)
    grad_part(2)
    first(2)

    @pl.when(away)
    def _():
        side_send(2)

    finish(0)
    deliver(0, 0)
    pass_on(1, 3)
    pass_on(2, 2)
    pass_on(1, 4)
    weights_of(3)
    forward_part(3)
    grad_part(3)
    first(3)
    first(5)

    @pl.when(home)
    def _():
        side_send(1)
        side_send(2)

    pass_on(2, 3)
    finish(1)
    token_part()
    pass_on(2, 4)
    pass_on(3, 2)
    pass_on(5, 2)
    side_merge()
    first(4)
    finish(2)
    deliver(1, 0)
    deliver(2, 0)
    pass_on(3, 3)
    pass_on(5, 3)
    pass_on(4, 2)
    pass_on(3, 4)
    pass_on(5, 4)
    pass_on(4, 3)
    gate_copy.wait_recv()
    gate_tok = gate_acc[0][:, :256] + gr[0:1]
    column = jnp.sum(jnp.where(named, gate_tok, 0.0), axis=1, keepdims=True)
    out_gate[...] = jnp.broadcast_to(column, (224, 128)).T[0:1]
    dx_copy.wait_recv()
    out_x[...] = (dxo[...] + dxr[...]).astype(BF16)

    finish(3)
    deliver(3, 0)
    finish(5)
    deliver(3, 1)
    pass_on(4, 4)
    finish(4)
    deliver(0, 1)

    def source(r):
        return ((y + r // 4) % 4) * 4 + (x + r % 4) % 4

    def arrive(other):
        remote(a2.at[other], a2.at[other], ps.at[0, 0, 0], pr.at[other], sibling).wait_recv()

    @pl.when(away)
    def _():
        arrive(place)

    for r in (4, 8, 12, 2, 6, 10, 14):
        arrive(source(r))

    total = a2[place].astype(F32)
    for r in (4, 8, 12, 2, 6, 10, 14):
        total = total + a2[source(r)].astype(F32)
    acc[...] = total

    @pl.when(yh == 0)
    def _():
        extra = acc[...]
        for r in (1, 5, 9, 13, 3, 7, 11, 15):
            arrive(source(r))
            extra = extra + a2[source(r)].astype(F32)
        acc[...] = extra

    for m, out in enumerate((out_g, out_u, out_d)):
        block = (acc[48 * m : 48 * m + 48] * factor).T
        out[...] = jnp.concatenate([block[:64], block[64:]], axis=1).astype(BF16)

    for copy in sib + [dx_copy, gate_copy]:
        copy.wait_send()
    for r in range(6):
        for way in range(2):
            for step in range(1, 5):
                if sends(RINGS[r], way, step):
                    ring_copy(r, way, step).wait_send()
    for t in (1, 2):
        for i in range(2):
            side_copy(t, i).wait_send()
    for j, h in ((0, 0), (1, 0), (2, 0), (3, 0), (0, 1), (3, 1)):
        for kk in range(2):
            if (j, kk) == (0, 0):

                @pl.when(jnp.logical_not(jnp.logical_and(home, yh == h)))
                def _():
                    deliver_copy(0, h, 0).wait_send()

            else:
                deliver_copy(j, h, kk).wait_send()

    @pl.when(away)
    def _():
        for copy in away_f():
            copy.wait_send()

    @pl.when(home)
    def _():
        for copy in ring_a() + ring_b() + ring_f():
            copy.wait_send()
        for t in range(TICKS):
            for copy in up_down(t):
                copy.wait_send()


def hand_over(*refs):
    copies = [
        pltpu.make_async_copy(refs[i], refs[5 + i], refs[10].at[i]) for i in range(5)
    ]
    for copy in copies:
        copy.start()
    for copy in copies:
        copy.wait()


def per_device(tokens, cotangent, slot_token, slot_gate, w_gate, w_up, w_down):
    factor = float(65536) ** (-0.5)
    vmem = pl.BlockSpec(memory_space=pltpu.VMEM)
    hbm = pl.BlockSpec(memory_space=pl.ANY)
    dma = pltpu.SemaphoreType.DMA
    outs = pl.pallas_call(
        lambda *refs: kernel(factor, *refs),
        out_shape=(
            jax.ShapeDtypeStruct((256, 2048), BF16),
            jax.ShapeDtypeStruct((1, 224), F32),
            jax.ShapeDtypeStruct((64, 96), BF16),
            jax.ShapeDtypeStruct((64, 96), BF16),
            jax.ShapeDtypeStruct((64, 96), BF16),
        ),
        in_specs=[hbm, hbm, vmem, vmem, hbm, hbm, hbm],
        out_specs=(vmem,) * 5,
        scratch_shapes=[
            pltpu.VMEM((512, 2048), BF16),
            pltpu.VMEM((512, 2048), BF16),
            pltpu.VMEM((2048, 512), BF16),
            pltpu.VMEM((2048, 512), BF16),
            pltpu.VMEM((2, 8, 256), F32),
            pltpu.VMEM((192, 512), F32),
            pltpu.VMEM((96, 512), F32),
            pltpu.VMEM((768, 2048), BF16),
            pltpu.VMEM((384, 2048), BF16),
            pltpu.VMEM((768, 512), BF16),
            pltpu.VMEM((96, 512), BF16),
            pltpu.VMEM((4, 8, 2, 288, 128), BF16),
            pltpu.VMEM((4, 2, 4, 2, 288, 128), BF16),
            pltpu.VMEM((4, 2, 288, 128), F32),
            pltpu.VMEM((2, 2, 8, 144, 128), BF16),
            pltpu.VMEM((4, 2, 2, 144, 128), BF16),
            pltpu.VMEM((16, 144, 128), BF16),
            pltpu.VMEM((144, 128), F32),
            pltpu.VMEM((256, 2048), F32),
            pltpu.VMEM((256, 2048), F32),
            pltpu.VMEM((256, 2048), F32),
            pltpu.VMEM((8, 256), F32),
            pltpu.VMEM((8, 256), F32),
            dma((7,)),
            dma((5,)),
            dma((5,)),
            dma((6, 2)),
            dma((8, 2)),
            dma((4, 2, 2)),
            dma((6, 2, 4)),
            dma((6, 2, 4)),
            dma((2, 2)),
            dma((2, 2)),
            dma((4, 2, 2)),
            dma((16,)),
        ],
        compiler_params=pltpu.CompilerParams(
            collective_id=0, has_side_effects=True, vmem_limit_bytes=56 << 20
        ),
        name="expert_backward",
    )(tokens, cotangent, slot_token.reshape(1, 224), slot_gate, w_gate, w_up, w_down)
    outs = pl.pallas_call(
        hand_over,
        out_shape=[jax.ShapeDtypeStruct(o.shape, o.dtype) for o in outs],
        in_specs=[vmem] * 5,
        out_specs=[hbm] * 5,
        scratch_shapes=[dma((5,))],
        name="hand_over",
    )(*outs)
    return (outs[0], outs[1].reshape(224), outs[2].T, outs[3].T, outs[4].T)


def solution(mesh):
    both = P(("dp", "blk"), None)
    flat = P(("dp", "blk"))
    rows = P("blk", None)
    block = P("blk", "dp")
    return jax.shard_map(
        per_device,
        mesh=mesh,
        in_specs=(both, both, flat, flat, rows, rows, rows),
        out_specs=(both, flat, block, block, block),
        check_vma=False,
    )
```

```python
import jax
import jax.numpy as jnp
from jax import lax
from jax.experimental import pallas as pl
from jax.experimental.pallas import tpu as pltpu
from jax.sharding import PartitionSpec as P

MESH = pl.DeviceIdType.MESH
F32 = jnp.float32
BF16 = jnp.bfloat16
TICKS = 4

RINGS = ((0, 0, 0), (1, 0, 1), (2, 0, 0), (3, 0, 0), (0, 1, 1), (3, 1, 1))
SHORT = (4,)
LONG = (3, 5)


def dot_nt(a, b):
    return lax.dot_general(a, b, (((1,), (1,)), ((), ())), preferred_element_type=F32)


def dot_nn(a, b):
    return lax.dot_general(a, b, (((1,), (0,)), ((), ())), preferred_element_type=F32)


def kernel(
    factor, tok, cot, slot, gate, wg, wu, wd,
    out_x, out_gate, out_g, out_u, out_d,
    xb, db, xt, dt, cb, ups, raws, wgu, wdn, dgs, qs, grad, recv, fin, side, pack, a2, acc, ox, dxs, dxr, gs, gr,
    loc_sem, sib_s, sib_r, ax_s, ay_s, ag_r, zs, zr, xs_, xr, ps, pr,
):
    dp, blk = lax.axis_index("dp"), lax.axis_index("blk")
    c, z, yh = dp % 2, (dp // 2) % 8, dp // 16
    x, yl = blk % 4, blk // 4
    y = yh * 2 + yl
    home = c == yl
    away = c != yl

    def device(xx, yy, zz, cc):
        return ((yy // 2) * 16 + zz * 2 + cc, (yy % 2) * 4 + xx)

    right, left = device((x + 1) % 4, y, z, c), device((x + 3) % 4, y, z, c)
    above, below = device(x, (y + 1) % 4, z, c), device(x, (y + 3) % 4, z, c)
    zside = (device(x, y, (z + 1) % 8, c), device(x, y, (z + 7) % 8, c))
    zfar = (device(x, y, (z + 2) % 8, c), device(x, y, (z + 6) % 8, c))
    sibling = device(x, y, z, 1 - c)
    place = y * 4 + x

    loads = [
        pltpu.make_async_copy(tok, xb.at[pl.ds(0, 256)], loc_sem.at[0]),
        pltpu.make_async_copy(cot, db.at[pl.ds(0, 256)], loc_sem.at[1]),
    ]
    wloads = [
        pltpu.make_async_copy(wg.at[pl.ds(0, 48)], wgu.at[pl.ds(0, 48)], loc_sem.at[2]),
        pltpu.make_async_copy(wu.at[pl.ds(0, 48)], wgu.at[pl.ds(48, 48)], loc_sem.at[3]),
        pltpu.make_async_copy(wg.at[pl.ds(48, 48)], wgu.at[pl.ds(96, 48)], loc_sem.at[4]),
        pltpu.make_async_copy(wu.at[pl.ds(48, 48)], wgu.at[pl.ds(144, 48)], loc_sem.at[5]),
        pltpu.make_async_copy(wd, wdn.at[pl.ds(0, 96)], loc_sem.at[6]),
    ]

    @pl.when(home)
    def _():
        for copy in wloads:
            copy.start()

    for copy in loads:
        copy.start()

    barrier = pltpu.get_barrier_semaphore()

    def greet(target):
        pl.semaphore_signal(barrier, inc=1, device_id=target, device_id_type=MESH)

    greet(zside[0])
    greet(zside[1])
    greet(zfar[0])
    greet(zfar[1])
    greet(sibling)

    def greet_plane(r, carry):
        other = (place + r) % 16
        greet(device(other % 4, other // 4, z, yl))
        return carry

    lax.fori_loop(1, 16, greet_plane, 0)

    @pl.when(away)
    def _():
        greet(above)
        greet(below)
        greet(right)
        greet(left)

    slots = jnp.broadcast_to(slot[...].astype(F32), (128, 224)).T[:, 0:1]
    gates = jnp.broadcast_to(gate[...].astype(F32).reshape(1, 224), (128, 224)).T[:, 0:1]
    token_of = lax.broadcasted_iota(jnp.int32, (224, 256), 1).astype(F32)
    named = token_of == slots
    cb[0] = jnp.broadcast_to(
        jnp.sum(jnp.where(named, gates, 0.0), axis=0, keepdims=True), (8, 256)
    )

    @pl.when(home)
    def _():
        for copy in wloads:
            copy.wait()

    for copy in loads:
        copy.wait()
    pl.semaphore_wait(barrier, jnp.where(home, 21, 23))

    def remote(src, dst, s_sem, r_sem, target):
        return pltpu.make_async_remote_copy(
            src_ref=src, dst_ref=dst, send_sem=s_sem, recv_sem=r_sem,
            device_id=target, device_id_type=MESH,
        )

    def unit(t, i):
        return (wgu.at[pl.ds(192 * t + 96 * i, 96)], wdn.at[pl.ds(96 * t + 48 * i, 48)])

    def send_unit(src, dst, sem, n, target):
        a, b = unit(*src), unit(*dst)
        return [
            remote(a[p], b[p], sem.at[n, p], ag_r.at[dst[0], dst[1], p], target)
            for p in range(2)
        ]

    def ring_a():
        return send_unit((0, 0), (1, 0), ax_s, 0, right) + send_unit((0, 1), (1, 1), ax_s, 1, left)

    def ring_b():
        return send_unit((0, 1), (2, 0), ax_s, 2, right) + send_unit((0, 0), (2, 1), ax_s, 3, left)

    def ring_f():
        return send_unit((1, 0), (3, 0), ax_s, 4, right) + send_unit((1, 1), (3, 1), ax_s, 5, left)

    def up_down(t):
        copies = send_unit((t, 0), (t, 0), ay_s, 2 * t, below) + send_unit((t, 1), (t, 1), ay_s, 2 * t + 1, above)
        return copies if t < 3 else copies[1::2]

    def away_f():
        return ring_f()[0::2]

    def start(copies):
        for copy in copies:
            copy.start()

    def wait_unit(t, i):
        for p in range(2):
            ref = unit(t, i)[p]
            remote(ref, ref, ax_s.at[0, p], ag_r.at[t, i, p], sibling).wait_recv()

    sib = [
        remote(xb.at[pl.ds(0, 256)], xb.at[pl.ds(256, 256)], sib_s.at[0], sib_r.at[0], sibling),
        remote(db.at[pl.ds(0, 256)], db.at[pl.ds(256, 256)], sib_s.at[1], sib_r.at[1], sibling),
        remote(cb.at[0], cb.at[1], sib_s.at[2], sib_r.at[2], sibling),
    ]

    @pl.when(home)
    def _():
        start(ring_a() + up_down(0))

    start(sib)

    gate_acc = [jnp.zeros((1, 512), F32)]

    def forward_part(t):
        top, low = 192 * t, 96 * t

        ups[...] = dot_nn(wgu[pl.ds(top, 192)], xt[...])
        raws[...] = dot_nn(wdn[pl.ds(low, 96)], dt[...])
        gu = ups[...]
        raw2 = raws[...]
        weight = jnp.concatenate([cb[0, 0:1], cb[1, 0:1]], axis=1)
        scaled = []
        for i in range(2):
            g = gu[96 * i : 96 * i + 48]
            u = gu[96 * i + 48 : 96 * i + 96]
            raw = raw2[48 * i : 48 * i + 48]
            sig = 1.0 / (1.0 + jnp.exp(-g))
            act = g * sig
            hid = act * u
            stored = hid.astype(BF16).astype(F32)
            gate_acc[0] = gate_acc[0] + jnp.sum(stored * raw, axis=0, keepdims=True)
            dh = weight * raw
            dgs[pl.ds(top + 96 * i, 48)] = (dh * u * sig * (1.0 + g * (1.0 - sig))).astype(BF16)
            dgs[pl.ds(top + 96 * i + 48, 48)] = (dh * act).astype(BF16)
            scaled.append((weight * hid).astype(BF16))
        qs[...] = jnp.concatenate(scaled, axis=0)

    def grad_part(t):
        q = qs[...]
        dgu = dgs[pl.ds(192 * t, 192)]

        for n in range(8):
            cols = slice(256 * n, 256 * n + 256)
            part = dot_nn(dgu, xb[:, cols]).astype(BF16)
            for k in range(2):
                lanes = slice(128 * k, 128 * k + 128)
                place_at = grad.at[t, 2 * (n % 4) + k, n // 4]
                place_at[0:96] = part[0:96, lanes]
                place_at[144:240] = part[96:192, lanes]
        for n in range(8):
            cols = slice(256 * n, 256 * n + 256)
            down = dot_nn(q, db[:, cols]).astype(BF16)
            for k in range(2):
                lanes = slice(128 * k, 128 * k + 128)
                place_at = grad.at[t, 2 * (n % 4) + k, n // 4]
                place_at[96:144] = down[0:48, lanes]
                place_at[240:288] = down[48:96, lanes]

    def has(r, way, step):
        return step > 1 or RINGS[r][2] == way

    def ring_copy(r, way, step):
        t, h, _ = RINGS[r]
        dest = (z + (1, 7)[way] * (5 - step)) % 8
        target = (zfar if (step == 1 and r not in LONG) or (step == 3 and r in SHORT) else zside)[way]
        return remote(
            grad.at[t, dest, h], recv.at[t, way, step - 1, h],
            zs.at[r, way, step - 1], zr.at[r, way, step - 1], target,
        )

    def first(r):
        for way in range(2):
            for step in (1, 2, 4) if r in SHORT else (1, 2):
                if has(r, way, step) and not (step == 2 and r in LONG and has(r, way, 1)):
                    ring_copy(r, way, step).start()

    def pass_on(r, step):
        t, h, _ = RINGS[r]
        if step == 4 and r in SHORT:
            return
        if step == 2 and r not in LONG:
            return
        for way in range(2):
            if step == 2 and not has(r, way, 1):
                continue
            dest = (z + (1, 7)[way] * (5 - step)) % 8
            ring_copy(r, way, step - 1).wait_recv()
            total = grad[t, dest, h].astype(F32) + recv[t, way, step - 2, h].astype(F32)
            if step == 3 and has(r, way, 1) and r not in LONG:
                ring_copy(r, way, 1).wait_recv()
                total = total + recv[t, way, 0, h].astype(F32)
            grad[t, dest, h] = total.astype(BF16)
            ring_copy(r, way, step).start()

    def finish(r):
        t, h, _ = RINGS[r]
        for way in range(2):
            ring_copy(r, way, 4).wait_recv()
        total = grad[t, z, h].astype(F32) + recv[t, 0, 3, h].astype(F32) + recv[t, 1, 3, h].astype(F32)
        if r in SHORT:
            for way in range(2):
                ring_copy(r, way, 3).wait_recv()
            total = total + recv[t, 0, 2, h].astype(F32) + recv[t, 1, 2, h].astype(F32)
        fin[t, h] = total

    def side_copy(t, i):
        return remote(
            grad.at[t, :, 1, pl.ds(144 * i, 144)], side.at[t - 1, i],
            xs_.at[t - 1, i], xr.at[t - 1, i], left if i == 0 else right,
        )

    def side_send(t):
        for i in range(2):
            side_copy(t, i).start()

    def side_merge():
        for t in (1, 2):
            for i in range(2):
                side_copy(t, i).wait_recv()
        for i in range(2):
            rows = pl.ds(144 * i, 144)
            for k in range(8):
                total = grad[0, k, 1, rows].astype(F32) + side[0, i, k].astype(F32) + side[1, 1 - i, k].astype(F32)
                grad[0, k, 1, rows] = total.astype(BF16)

    low_lanes = lax.broadcasted_iota(jnp.int32, (144, 128), 1) < 64
    halves = (((0, 0), (0, 1)), ((1, 0), (2, 0)), ((2, 1), (1, 1)), ((3, 0), (3, 1)))
    offset = (0, 3, 1, 2)

    def rows_of(t, i, h):
        return fin[t, h, pl.ds(144 * i, 144)]

    def deliver_copy(j, h, kk):
        k = (c + kk) % 2
        target = device((x + offset[j]) % 4, 2 * h + c, z, k)
        return remote(pack.at[j, h, k], a2.at[place], ps.at[j, h, kk], pr.at[place], target)

    def deliver(j, h):
        a, b = rows_of(*halves[j][0], h), rows_of(*halves[j][1], h)
        pack[j, h, 0] = jnp.where(low_lanes, a, pltpu.roll(b, 64, 1)).astype(BF16)
        pack[j, h, 1] = jnp.where(low_lanes, pltpu.roll(a, 64, 1), b).astype(BF16)
        for kk in range(2):
            if (j, kk) == (0, 0):
                mine = jnp.logical_and(home, yh == h)

                @pl.when(mine)
                def _():
                    a2[place] = pack[0, h, c]

                @pl.when(jnp.logical_not(mine))
                def _():
                    deliver_copy(0, h, 0).start()

            else:
                deliver_copy(j, h, kk).start()

    dx_copy = remote(dxs, dxr, sib_s.at[3], sib_r.at[3], sibling)
    gate_copy = remote(gs, gr, sib_s.at[4], sib_r.at[4], sibling)

    def sibling_rows(k):
        left_side = dgs[pl.ds(384 * k, 384), 256:512].T
        for n in range(8):
            cols = slice(256 * n, 256 * n + 256)
            part = dot_nn(left_side, wgu[pl.ds(384 * k, 384), cols])
            dxs[:, cols] = part if k == 0 else dxs[:, cols] + part

    def own_rows():
        left_side = dgs[:, 0:256].T
        for n in range(8):
            cols = slice(256 * n, 256 * n + 256)
            ox[:, cols] = (dot_nn(left_side, wgu[:, cols]) + dxr[:, cols]).astype(BF16)

    def away_weights(t):
        wait_unit(t, 0)
        wait_unit(t, 1)
        if t == 1:
            start(away_f())

    def home_weights(t):
        for i in range(2):
            wait_unit(t, i)
            if t == 1:
                start(ring_f()[2 * i : 2 * i + 2])
            start(send_unit((t, i), (t, i), ay_s, 2 * t + i, (below, above)[i])[1 if t == 3 else 0 :])

    xt[:, 0:256] = xb[0:256].T
    dt[:, 0:256] = db[0:256].T
    for copy in sib:
        copy.wait_recv()
    xt[:, 256:512] = xb[256:512].T
    dt[:, 256:512] = db[256:512].T

    @pl.when(away)
    def _():
        away_weights(0)

    forward_part(0)

    @pl.when(home)
    def _():
        start(ring_b())

    grad_part(0)
    first(0)

    @pl.when(home)
    def _():
        home_weights(1)

    @pl.when(away)
    def _():
        pass_on(0, 2)
        pass_on(0, 3)
        away_weights(1)

    forward_part(1)
    grad_part(1)
    first(1)

    @pl.when(home)
    def _():
        pass_on(0, 2)
        pass_on(0, 3)
        home_weights(2)
        pass_on(1, 2)
        pass_on(0, 4)
        pass_on(1, 3)

    @pl.when(away)
    def _():
        side_send(1)
        pass_on(0, 4)
        pass_on(1, 2)
        pass_on(1, 3)

    sibling_rows(0)

    @pl.when(away)
    def _():
        away_weights(2)

    forward_part(2)
    grad_part(2)
    first(2)

    @pl.when(home)
    def _():
        side_send(1)
        pass_on(1, 4)
        home_weights(3)
        finish(0)
        deliver(0, 0)
        pass_on(2, 2)
        pass_on(2, 3)

    @pl.when(away)
    def _():
        side_send(2)
        pass_on(1, 4)
        away_weights(3)

    forward_part(3)
    grad_part(3)
    first(3)
    first(5)

    @pl.when(home)
    def _():
        side_send(2)
        pass_on(2, 4)

    @pl.when(away)
    def _():
        pass_on(2, 2)
        finish(0)
        deliver(0, 0)
        pass_on(2, 3)

    gs[...] = jnp.broadcast_to(gate_acc[0][:, 256:], (8, 256))
    gate_copy.start()
    finish(1)
    sibling_rows(1)
    dx_copy.start()
    pass_on(3, 2)
    pass_on(5, 2)

    @pl.when(away)
    def _():
        pass_on(2, 4)

    pass_on(3, 3)
    pass_on(5, 3)
    side_merge()
    first(4)
    pass_on(3, 4)
    pass_on(5, 4)
    finish(2)
    deliver(1, 0)
    deliver(2, 0)
    pass_on(4, 3)
    finish(3)
    deliver(3, 0)
    finish(5)
    deliver(3, 1)
    pass_on(4, 4)
    finish(4)
    deliver(0, 1)
    gate_copy.wait_recv()
    gate_tok = gate_acc[0][:, :256] + gr[0:1]
    column = jnp.sum(jnp.where(named, gate_tok, 0.0), axis=1, keepdims=True)
    out_gate[...] = jnp.broadcast_to(column, (224, 128)).T[0:1]
    dx_copy.wait_recv()
    own_rows()
    out_copy = pltpu.make_async_copy(ox, out_x, loc_sem.at[7])
    out_copy.start()
    for copy in sib + [dx_copy, gate_copy]:
        copy.wait_send()
    for r in range(6):
        for way in range(2):
            for step in range(1, 5):
                if has(r, way, step):
                    ring_copy(r, way, step).wait_send()
    for t in (1, 2):
        for i in range(2):
            side_copy(t, i).wait_send()
    @pl.when(away)
    def _():
        for copy in away_f():
            copy.wait_send()

    @pl.when(home)
    def _():
        for copy in ring_a() + ring_b() + ring_f():
            copy.wait_send()
        for t in range(TICKS):
            for copy in up_down(t):
                copy.wait_send()


    def source(r):
        return ((y + r // 4) % 4) * 4 + (x + r % 4) % 4

    def arrive(other):
        remote(a2.at[other], a2.at[other], ps.at[0, 0, 0], pr.at[other], sibling).wait_recv()

    @pl.when(away)
    def _():
        arrive(place)

    for r in (4, 8, 12, 2, 6, 10, 14):
        arrive(source(r))

    total = a2[place].astype(F32)
    for r in (4, 8, 12, 2, 6, 10, 14):
        total = total + a2[source(r)].astype(F32)
    acc[...] = total

    @pl.when(yh == 0)
    def _():
        extra = acc[...]
        for r in (1, 5, 9, 13, 3, 7, 11, 15):
            arrive(source(r))
            extra = extra + a2[source(r)].astype(F32)
        acc[...] = extra

    for m, out in enumerate((out_g, out_u, out_d)):
        block = (acc[48 * m : 48 * m + 48] * factor).T
        out[...] = jnp.concatenate([block[:64], block[64:]], axis=1).astype(BF16)

    for j, h in ((0, 0), (1, 0), (2, 0), (3, 0), (0, 1), (3, 1)):
        for kk in range(2):
            if (j, kk) == (0, 0):

                @pl.when(jnp.logical_not(jnp.logical_and(home, yh == h)))
                def _():
                    deliver_copy(0, h, 0).wait_send()

            else:
                deliver_copy(j, h, kk).wait_send()
    out_copy.wait()


def hand_over(*refs):
    ins, outs, held = refs[0:5], refs[5:10], refs[10:15]
    in_sem, out_sem = refs[15], refs[16]

    def pieces(src, dst):
        whole = [(src[0].at[pl.ds(64 * i, 64)], dst[0].at[pl.ds(64 * i, 64)]) for i in range(4)]
        return whole + list(zip(src[1:], dst[1:]))

    loads = [pltpu.make_async_copy(p, q, in_sem.at[i]) for i, (p, q) in enumerate(pieces(ins, held))]
    stores = [pltpu.make_async_copy(p, q, out_sem.at[i]) for i, (p, q) in enumerate(pieces(held, outs))]
    for copy in loads:
        copy.start()
    for i in range(8):
        loads[i].wait()
        stores[i].start()
    for copy in stores:
        copy.wait()


def per_device(tokens, cotangent, slot_token, slot_gate, w_gate, w_up, w_down):
    factor = float(65536) ** (-0.5)
    vmem = pl.BlockSpec(memory_space=pltpu.VMEM)
    hbm = pl.BlockSpec(memory_space=pl.ANY)
    dma = pltpu.SemaphoreType.DMA
    outs = pl.pallas_call(
        lambda *refs: kernel(factor, *refs),
        out_shape=(
            jax.ShapeDtypeStruct((256, 2048), BF16),
            jax.ShapeDtypeStruct((1, 224), F32),
            jax.ShapeDtypeStruct((64, 96), BF16),
            jax.ShapeDtypeStruct((64, 96), BF16),
            jax.ShapeDtypeStruct((64, 96), BF16),
        ),
        in_specs=[hbm, hbm, vmem, vmem, hbm, hbm, hbm],
        out_specs=(hbm,) + (vmem,) * 4,
        scratch_shapes=[
            pltpu.VMEM((512, 2048), BF16),
            pltpu.VMEM((512, 2048), BF16),
            pltpu.VMEM((2048, 512), BF16),
            pltpu.VMEM((2048, 512), BF16),
            pltpu.VMEM((2, 8, 256), F32),
            pltpu.VMEM((192, 512), F32),
            pltpu.VMEM((96, 512), F32),
            pltpu.VMEM((768, 2048), BF16),
            pltpu.VMEM((384, 2048), BF16),
            pltpu.VMEM((768, 512), BF16),
            pltpu.VMEM((96, 512), BF16),
            pltpu.VMEM((4, 8, 2, 288, 128), BF16),
            pltpu.VMEM((4, 2, 4, 2, 288, 128), BF16),
            pltpu.VMEM((4, 2, 288, 128), F32),
            pltpu.VMEM((2, 2, 8, 144, 128), BF16),
            pltpu.VMEM((4, 2, 2, 144, 128), BF16),
            pltpu.VMEM((16, 144, 128), BF16),
            pltpu.VMEM((144, 128), F32),
            pltpu.VMEM((256, 2048), BF16),
            pltpu.VMEM((256, 2048), F32),
            pltpu.VMEM((256, 2048), F32),
            pltpu.VMEM((8, 256), F32),
            pltpu.VMEM((8, 256), F32),
            dma((8,)),
            dma((5,)),
            dma((5,)),
            dma((6, 2)),
            dma((8, 2)),
            dma((4, 2, 2)),
            dma((6, 2, 4)),
            dma((6, 2, 4)),
            dma((2, 2)),
            dma((2, 2)),
            dma((4, 2, 2)),
            dma((16,)),
        ],
        compiler_params=pltpu.CompilerParams(
            collective_id=0, has_side_effects=True, vmem_limit_bytes=56 << 20
        ),
        name="expert_backward",
    )(tokens, cotangent, slot_token.reshape(1, 224), slot_gate, w_gate, w_up, w_down)
    outs = pl.pallas_call(
        hand_over,
        out_shape=[jax.ShapeDtypeStruct(o.shape, o.dtype) for o in outs],
        in_specs=[hbm] * 5,
        out_specs=[hbm] * 5,
        scratch_shapes=[pltpu.VMEM(o.shape, o.dtype) for o in outs] + [dma((8,)), dma((8,))],
        name="hand_over",
    )(*outs)
    return (outs[0], outs[1].reshape(224), outs[2].T, outs[3].T, outs[4].T)


def solution(mesh):
    both = P(("dp", "blk"), None)
    flat = P(("dp", "blk"))
    rows = P("blk", None)
    block = P("blk", "dp")
    return jax.shard_map(
        per_device,
        mesh=mesh,
        in_specs=(both, both, flat, flat, rows, rows, rows),
        out_specs=(both, flat, block, block, block),
        check_vma=False,
    )
```

```python
import jax
import jax.numpy as jnp
from jax import lax
from jax.experimental import pallas as pl
from jax.experimental.pallas import tpu as pltpu
from jax.sharding import PartitionSpec as P

MESH = pl.DeviceIdType.MESH
F32 = jnp.float32
BF16 = jnp.bfloat16
TICKS = 4

RINGS = ((0, 0, 0), (1, 0, 1), (2, 0, 0), (3, 0, 0), (0, 1, 1), (3, 1, 1))
SHORT = (4,)
LONG = (3, 5)


def dot_nt(a, b):
    return lax.dot_general(a, b, (((1,), (1,)), ((), ())), preferred_element_type=F32)


def dot_nn(a, b):
    return lax.dot_general(a, b, (((1,), (0,)), ((), ())), preferred_element_type=F32)


def kernel(
    factor, tok, cot, slot, gate, wg, wu, wd,
    out_x, out_gate, out_g, out_u, out_d,
    xb, db, xt, dt, cb, ups, raws, wgu, wdn, dgs, qs, grad, recv, fin, side, pack, a2, acc, ox, dxs, dxr, gs, gr,
    loc_sem, sib_s, sib_r, ax_s, ay_s, ag_r, zs, zr, xs_, xr, ps, pr,
):
    dp, blk = lax.axis_index("dp"), lax.axis_index("blk")
    c, z, yh = dp % 2, (dp // 2) % 8, dp // 16
    x, yl = blk % 4, blk // 4
    y = yh * 2 + yl
    home = c == yl
    away = c != yl

    def device(xx, yy, zz, cc):
        return ((yy // 2) * 16 + zz * 2 + cc, (yy % 2) * 4 + xx)

    right, left = device((x + 1) % 4, y, z, c), device((x + 3) % 4, y, z, c)
    above, below = device(x, (y + 1) % 4, z, c), device(x, (y + 3) % 4, z, c)
    zside = (device(x, y, (z + 1) % 8, c), device(x, y, (z + 7) % 8, c))
    zfar = (device(x, y, (z + 2) % 8, c), device(x, y, (z + 6) % 8, c))
    sibling = device(x, y, z, 1 - c)
    place = y * 4 + x

    loads = [
        pltpu.make_async_copy(tok, xb.at[pl.ds(0, 256)], loc_sem.at[0]),
        pltpu.make_async_copy(cot, db.at[pl.ds(0, 256)], loc_sem.at[1]),
    ]
    wloads = [
        pltpu.make_async_copy(wg.at[pl.ds(0, 48)], wgu.at[pl.ds(0, 48)], loc_sem.at[2]),
        pltpu.make_async_copy(wu.at[pl.ds(0, 48)], wgu.at[pl.ds(48, 48)], loc_sem.at[3]),
        pltpu.make_async_copy(wg.at[pl.ds(48, 48)], wgu.at[pl.ds(96, 48)], loc_sem.at[4]),
        pltpu.make_async_copy(wu.at[pl.ds(48, 48)], wgu.at[pl.ds(144, 48)], loc_sem.at[5]),
        pltpu.make_async_copy(wd, wdn.at[pl.ds(0, 96)], loc_sem.at[6]),
    ]

    @pl.when(home)
    def _():
        for copy in wloads:
            copy.start()

    for copy in loads:
        copy.start()

    barrier = pltpu.get_barrier_semaphore()

    def greet(target):
        pl.semaphore_signal(barrier, inc=1, device_id=target, device_id_type=MESH)

    greet(zside[0])
    greet(zside[1])
    greet(zfar[0])
    greet(zfar[1])
    greet(sibling)

    def greet_plane(r, carry):
        other = (place + r) % 16
        greet(device(other % 4, other // 4, z, yl))
        return carry

    lax.fori_loop(1, 16, greet_plane, 0)

    @pl.when(away)
    def _():
        greet(above)
        greet(below)
        greet(right)
        greet(left)

    slots = jnp.broadcast_to(slot[...].astype(F32), (128, 224)).T[:, 0:1]
    gates = jnp.broadcast_to(gate[...].astype(F32).reshape(1, 224), (128, 224)).T[:, 0:1]
    token_of = lax.broadcasted_iota(jnp.int32, (224, 256), 1).astype(F32)
    named = token_of == slots
    cb[0] = jnp.broadcast_to(
        jnp.sum(jnp.where(named, gates, 0.0), axis=0, keepdims=True), (8, 256)
    )

    @pl.when(home)
    def _():
        for copy in wloads:
            copy.wait()

    for copy in loads:
        copy.wait()
    pl.semaphore_wait(barrier, jnp.where(home, 21, 23))

    def remote(src, dst, s_sem, r_sem, target):
        return pltpu.make_async_remote_copy(
            src_ref=src, dst_ref=dst, send_sem=s_sem, recv_sem=r_sem,
            device_id=target, device_id_type=MESH,
        )

    def unit(t, i):
        return (wgu.at[pl.ds(192 * t + 96 * i, 96)], wdn.at[pl.ds(96 * t + 48 * i, 48)])

    def send_unit(src, dst, sem, n, target):
        a, b = unit(*src), unit(*dst)
        return [
            remote(a[p], b[p], sem.at[n, p], ag_r.at[dst[0], dst[1], p], target)
            for p in range(2)
        ]

    def ring_a():
        return send_unit((0, 0), (1, 0), ax_s, 0, right) + send_unit((0, 1), (1, 1), ax_s, 1, left)

    def ring_b():
        return send_unit((0, 1), (2, 0), ax_s, 2, right) + send_unit((0, 0), (2, 1), ax_s, 3, left)

    def ring_f():
        return send_unit((1, 0), (3, 0), ax_s, 4, right) + send_unit((1, 1), (3, 1), ax_s, 5, left)

    def up_down(t):
        copies = send_unit((t, 0), (t, 0), ay_s, 2 * t, below) + send_unit((t, 1), (t, 1), ay_s, 2 * t + 1, above)
        return copies if t < 3 else copies[1::2]

    def away_f():
        return ring_f()[0::2]

    def start(copies):
        for copy in copies:
            copy.start()

    def wait_unit(t, i):
        for p in range(2):
            ref = unit(t, i)[p]
            remote(ref, ref, ax_s.at[0, p], ag_r.at[t, i, p], sibling).wait_recv()

    sib = [
        remote(xb.at[pl.ds(0, 256)], xb.at[pl.ds(256, 256)], sib_s.at[0], sib_r.at[0], sibling),
        remote(db.at[pl.ds(0, 256)], db.at[pl.ds(256, 256)], sib_s.at[1], sib_r.at[1], sibling),
        remote(cb.at[0], cb.at[1], sib_s.at[2], sib_r.at[2], sibling),
    ]

    @pl.when(home)
    def _():
        start(ring_a() + up_down(0))

    start(sib)

    gate_acc = [jnp.zeros((1, 512), F32)]

    def forward_part(t):
        top, low = 192 * t, 96 * t

        ups[...] = dot_nn(wgu[pl.ds(top, 192)], xt[...])
        raws[...] = dot_nn(wdn[pl.ds(low, 96)], dt[...])
        gu = ups[...]
        raw2 = raws[...]
        weight = jnp.concatenate([cb[0, 0:1], cb[1, 0:1]], axis=1)
        scaled = []
        for i in range(2):
            g = gu[96 * i : 96 * i + 48]
            u = gu[96 * i + 48 : 96 * i + 96]
            raw = raw2[48 * i : 48 * i + 48]
            sig = 1.0 / (1.0 + jnp.exp(-g))
            act = g * sig
            hid = act * u
            stored = hid.astype(BF16).astype(F32)
            gate_acc[0] = gate_acc[0] + jnp.sum(stored * raw, axis=0, keepdims=True)
            dh = weight * raw
            dgs[pl.ds(top + 96 * i, 48)] = (dh * u * sig * (1.0 + g * (1.0 - sig))).astype(BF16)
            dgs[pl.ds(top + 96 * i + 48, 48)] = (dh * act).astype(BF16)
            scaled.append((weight * hid).astype(BF16))
        qs[...] = jnp.concatenate(scaled, axis=0)

    def grad_part(t):
        q = qs[...]
        dgu = dgs[pl.ds(192 * t, 192)]

        for n in range(8):
            cols = slice(256 * n, 256 * n + 256)
            part = dot_nn(dgu, xb[:, cols]).astype(BF16)
            for k in range(2):
                lanes = slice(128 * k, 128 * k + 128)
                place_at = grad.at[t, 2 * (n % 4) + k, n // 4]
                place_at[0:96] = part[0:96, lanes]
                place_at[144:240] = part[96:192, lanes]
        for n in range(8):
            cols = slice(256 * n, 256 * n + 256)
            down = dot_nn(q, db[:, cols]).astype(BF16)
            for k in range(2):
                lanes = slice(128 * k, 128 * k + 128)
                place_at = grad.at[t, 2 * (n % 4) + k, n // 4]
                place_at[96:144] = down[0:48, lanes]
                place_at[240:288] = down[48:96, lanes]

    def has(r, way, step):
        return step > 1 or RINGS[r][2] == way

    def ring_copy(r, way, step):
        t, h, _ = RINGS[r]
        dest = (z + (1, 7)[way] * (5 - step)) % 8
        target = (zfar if (step == 1 and r not in LONG) or (step == 3 and r in SHORT) else zside)[way]
        return remote(
            grad.at[t, dest, h], recv.at[t, way, step - 1, h],
            zs.at[r, way, step - 1], zr.at[r, way, step - 1], target,
        )

    def first(r):
        for way in range(2):
            for step in (1, 2, 4) if r in SHORT else (1, 2):
                if has(r, way, step) and not (step == 2 and r in LONG and has(r, way, 1)):
                    ring_copy(r, way, step).start()

    def pass_on(r, step):
        t, h, _ = RINGS[r]
        if step == 4 and r in SHORT:
            return
        if step == 2 and r not in LONG:
            return
        for way in range(2):
            if step == 2 and not has(r, way, 1):
                continue
            dest = (z + (1, 7)[way] * (5 - step)) % 8
            ring_copy(r, way, step - 1).wait_recv()
            total = grad[t, dest, h].astype(F32) + recv[t, way, step - 2, h].astype(F32)
            if step == 3 and has(r, way, 1) and r not in LONG:
                ring_copy(r, way, 1).wait_recv()
                total = total + recv[t, way, 0, h].astype(F32)
            grad[t, dest, h] = total.astype(BF16)
            ring_copy(r, way, step).start()

    def finish(r):
        t, h, _ = RINGS[r]
        for way in range(2):
            ring_copy(r, way, 4).wait_recv()
        total = grad[t, z, h].astype(F32) + recv[t, 0, 3, h].astype(F32) + recv[t, 1, 3, h].astype(F32)
        if r in SHORT:
            for way in range(2):
                ring_copy(r, way, 3).wait_recv()
            total = total + recv[t, 0, 2, h].astype(F32) + recv[t, 1, 2, h].astype(F32)
        fin[t, h] = total

    def side_copy(t, i):
        return remote(
            grad.at[t, :, 1, pl.ds(144 * i, 144)], side.at[t - 1, i],
            xs_.at[t - 1, i], xr.at[t - 1, i], left if i == 0 else right,
        )

    def side_send(t):
        for i in range(2):
            side_copy(t, i).start()

    def side_merge():
        for t in (1, 2):
            for i in range(2):
                side_copy(t, i).wait_recv()
        for i in range(2):
            rows = pl.ds(144 * i, 144)
            for k in range(8):
                total = grad[0, k, 1, rows].astype(F32) + side[0, i, k].astype(F32) + side[1, 1 - i, k].astype(F32)
                grad[0, k, 1, rows] = total.astype(BF16)

    low_lanes = lax.broadcasted_iota(jnp.int32, (144, 128), 1) < 64
    halves = (((0, 0), (0, 1)), ((1, 0), (2, 0)), ((2, 1), (1, 1)), ((3, 0), (3, 1)))
    offset = (0, 3, 1, 2)

    def rows_of(t, i, h):
        return fin[t, h, pl.ds(144 * i, 144)]

    def deliver_copy(j, h, kk):
        k = (c + kk) % 2
        target = device((x + offset[j]) % 4, 2 * h + c, z, k)
        return remote(pack.at[j, h, k], a2.at[place], ps.at[j, h, kk], pr.at[place], target)

    def deliver(j, h):
        a, b = rows_of(*halves[j][0], h), rows_of(*halves[j][1], h)
        pack[j, h, 0] = jnp.where(low_lanes, a, pltpu.roll(b, 64, 1)).astype(BF16)
        pack[j, h, 1] = jnp.where(low_lanes, pltpu.roll(a, 64, 1), b).astype(BF16)
        for kk in range(2):
            if (j, kk) == (0, 0):
                mine = jnp.logical_and(home, yh == h)

                @pl.when(mine)
                def _():
                    a2[place] = pack[0, h, c]

                @pl.when(jnp.logical_not(mine))
                def _():
                    deliver_copy(0, h, 0).start()

            else:
                deliver_copy(j, h, kk).start()

    dx_copy = remote(dxs, dxr, sib_s.at[3], sib_r.at[3], sibling)
    gate_copy = remote(gs, gr, sib_s.at[4], sib_r.at[4], sibling)

    def sibling_rows(k):
        left_side = dgs[pl.ds(384 * k, 384), 256:512].T
        for n in range(8):
            cols = slice(256 * n, 256 * n + 256)
            part = dot_nn(left_side, wgu[pl.ds(384 * k, 384), cols])
            dxs[:, cols] = part if k == 0 else dxs[:, cols] + part

    def own_rows():
        left_side = dgs[:, 0:256].T
        for n in range(8):
            cols = slice(256 * n, 256 * n + 256)
            ox[:, cols] = (dot_nn(left_side, wgu[:, cols]) + dxr[:, cols]).astype(BF16)

    def away_weights(t):
        wait_unit(t, 0)
        wait_unit(t, 1)
        if t == 1:
            start(away_f())

    def home_weights(t):
        for i in range(2):
            wait_unit(t, i)
            if t == 1:
                start(ring_f()[2 * i : 2 * i + 2])
            start(send_unit((t, i), (t, i), ay_s, 2 * t + i, (below, above)[i])[1 if t == 3 else 0 :])

    xt[:, 0:256] = xb[0:256].T
    dt[:, 0:256] = db[0:256].T
    for copy in sib:
        copy.wait_recv()
    xt[:, 256:512] = xb[256:512].T
    dt[:, 256:512] = db[256:512].T

    @pl.when(away)
    def _():
        away_weights(0)

    forward_part(0)

    @pl.when(home)
    def _():
        start(ring_b())

    grad_part(0)
    first(0)

    @pl.when(home)
    def _():
        home_weights(1)

    @pl.when(away)
    def _():
        pass_on(0, 2)
        pass_on(0, 3)
        away_weights(1)

    forward_part(1)
    grad_part(1)
    first(1)

    @pl.when(home)
    def _():
        pass_on(0, 2)
        pass_on(0, 3)
        home_weights(2)
        side_send(1)
        pass_on(1, 2)
        pass_on(0, 4)
        pass_on(1, 3)

    @pl.when(away)
    def _():
        side_send(1)
        pass_on(0, 4)
        pass_on(1, 2)
        pass_on(1, 3)

    sibling_rows(0)

    @pl.when(away)
    def _():
        away_weights(2)

    forward_part(2)
    grad_part(2)
    first(2)

    @pl.when(home)
    def _():
        pass_on(1, 4)
        home_weights(3)
        side_send(2)
        finish(0)
        deliver(0, 0)
        pass_on(2, 2)
        pass_on(2, 3)

    @pl.when(away)
    def _():
        side_send(2)
        pass_on(1, 4)
        away_weights(3)

    forward_part(3)
    grad_part(3)
    first(3)
    first(5)

    @pl.when(home)
    def _():
        pass_on(2, 4)

    @pl.when(away)
    def _():
        pass_on(2, 2)
        finish(0)
        deliver(0, 0)
        pass_on(2, 3)

    gs[...] = jnp.broadcast_to(gate_acc[0][:, 256:], (8, 256))
    gate_copy.start()
    finish(1)
    sibling_rows(1)
    dx_copy.start()
    pass_on(3, 2)
    pass_on(5, 2)

    @pl.when(away)
    def _():
        pass_on(2, 4)

    pass_on(3, 3)
    pass_on(5, 3)
    side_merge()
    first(4)
    pass_on(3, 4)
    pass_on(5, 4)
    finish(2)
    deliver(1, 0)
    deliver(2, 0)
    pass_on(4, 3)
    finish(3)
    deliver(3, 0)
    finish(5)
    deliver(3, 1)
    pass_on(4, 4)
    finish(4)
    deliver(0, 1)
    gate_copy.wait_recv()
    gate_tok = gate_acc[0][:, :256] + gr[0:1]
    column = jnp.sum(jnp.where(named, gate_tok, 0.0), axis=1, keepdims=True)
    out_gate[...] = jnp.broadcast_to(column, (224, 128)).T[0:1]
    dx_copy.wait_recv()
    own_rows()
    out_copy = pltpu.make_async_copy(ox, out_x, loc_sem.at[7])
    out_copy.start()
    for copy in sib + [dx_copy, gate_copy]:
        copy.wait_send()
    for r in range(6):
        for way in range(2):
            for step in range(1, 5):
                if has(r, way, step):
                    ring_copy(r, way, step).wait_send()
    for t in (1, 2):
        for i in range(2):
            side_copy(t, i).wait_send()
    @pl.when(away)
    def _():
        for copy in away_f():
            copy.wait_send()

    @pl.when(home)
    def _():
        for copy in ring_a() + ring_b() + ring_f():
            copy.wait_send()
        for t in range(TICKS):
            for copy in up_down(t):
                copy.wait_send()


    def source(r):
        return ((y + r // 4) % 4) * 4 + (x + r % 4) % 4

    def arrive(other):
        remote(a2.at[other], a2.at[other], ps.at[0, 0, 0], pr.at[other], sibling).wait_recv()

    @pl.when(away)
    def _():
        arrive(place)

    for r in (4, 8, 12, 2, 6, 10, 14):
        arrive(source(r))

    total = a2[place].astype(F32)
    for r in (4, 8, 12, 2, 6, 10, 14):
        total = total + a2[source(r)].astype(F32)
    acc[...] = total

    @pl.when(yh == 0)
    def _():
        extra = acc[...]
        for r in (1, 5, 9, 13, 3, 7, 11, 15):
            arrive(source(r))
            extra = extra + a2[source(r)].astype(F32)
        acc[...] = extra

    for m, out in enumerate((out_g, out_u, out_d)):
        block = (acc[48 * m : 48 * m + 48] * factor).T
        out[...] = jnp.concatenate([block[:64], block[64:]], axis=1).astype(BF16)

    for j, h in ((0, 0), (1, 0), (2, 0), (3, 0), (0, 1), (3, 1)):
        for kk in range(2):
            if (j, kk) == (0, 0):

                @pl.when(jnp.logical_not(jnp.logical_and(home, yh == h)))
                def _():
                    deliver_copy(0, h, 0).wait_send()

            else:
                deliver_copy(j, h, kk).wait_send()
    out_copy.wait()


def hand_over(*refs):
    ins, outs, held = refs[0:5], refs[5:10], refs[10:15]
    in_sem, out_sem = refs[15], refs[16]

    def pieces(src, dst):
        whole = [(src[0].at[pl.ds(64 * i, 64)], dst[0].at[pl.ds(64 * i, 64)]) for i in range(4)]
        return whole + list(zip(src[1:], dst[1:]))

    loads = [pltpu.make_async_copy(p, q, in_sem.at[i]) for i, (p, q) in enumerate(pieces(ins, held))]
    stores = [pltpu.make_async_copy(p, q, out_sem.at[i]) for i, (p, q) in enumerate(pieces(held, outs))]
    for copy in loads:
        copy.start()
    for i in range(8):
        loads[i].wait()
        stores[i].start()
    for copy in stores:
        copy.wait()


def per_device(tokens, cotangent, slot_token, slot_gate, w_gate, w_up, w_down):
    factor = float(65536) ** (-0.5)
    vmem = pl.BlockSpec(memory_space=pltpu.VMEM)
    hbm = pl.BlockSpec(memory_space=pl.ANY)
    dma = pltpu.SemaphoreType.DMA
    outs = pl.pallas_call(
        lambda *refs: kernel(factor, *refs),
        out_shape=(
            jax.ShapeDtypeStruct((256, 2048), BF16),
            jax.ShapeDtypeStruct((1, 224), F32),
            jax.ShapeDtypeStruct((64, 96), BF16),
            jax.ShapeDtypeStruct((64, 96), BF16),
            jax.ShapeDtypeStruct((64, 96), BF16),
        ),
        in_specs=[hbm, hbm, vmem, vmem, hbm, hbm, hbm],
        out_specs=(hbm,) + (vmem,) * 4,
        scratch_shapes=[
            pltpu.VMEM((512, 2048), BF16),
            pltpu.VMEM((512, 2048), BF16),
            pltpu.VMEM((2048, 512), BF16),
            pltpu.VMEM((2048, 512), BF16),
            pltpu.VMEM((2, 8, 256), F32),
            pltpu.VMEM((192, 512), F32),
            pltpu.VMEM((96, 512), F32),
            pltpu.VMEM((768, 2048), BF16),
            pltpu.VMEM((384, 2048), BF16),
            pltpu.VMEM((768, 512), BF16),
            pltpu.VMEM((96, 512), BF16),
            pltpu.VMEM((4, 8, 2, 288, 128), BF16),
            pltpu.VMEM((4, 2, 4, 2, 288, 128), BF16),
            pltpu.VMEM((4, 2, 288, 128), F32),
            pltpu.VMEM((2, 2, 8, 144, 128), BF16),
            pltpu.VMEM((4, 2, 2, 144, 128), BF16),
            pltpu.VMEM((16, 144, 128), BF16),
            pltpu.VMEM((144, 128), F32),
            pltpu.VMEM((256, 2048), BF16),
            pltpu.VMEM((256, 2048), F32),
            pltpu.VMEM((256, 2048), F32),
            pltpu.VMEM((8, 256), F32),
            pltpu.VMEM((8, 256), F32),
            dma((8,)),
            dma((5,)),
            dma((5,)),
            dma((6, 2)),
            dma((8, 2)),
            dma((4, 2, 2)),
            dma((6, 2, 4)),
            dma((6, 2, 4)),
            dma((2, 2)),
            dma((2, 2)),
            dma((4, 2, 2)),
            dma((16,)),
        ],
        compiler_params=pltpu.CompilerParams(
            collective_id=0, has_side_effects=True, vmem_limit_bytes=56 << 20
        ),
        name="expert_backward",
    )(tokens, cotangent, slot_token.reshape(1, 224), slot_gate, w_gate, w_up, w_down)
    outs = pl.pallas_call(
        hand_over,
        out_shape=[jax.ShapeDtypeStruct(o.shape, o.dtype) for o in outs],
        in_specs=[hbm] * 5,
        out_specs=[hbm] * 5,
        scratch_shapes=[pltpu.VMEM(o.shape, o.dtype) for o in outs] + [dma((8,)), dma((8,))],
        name="hand_over",
    )(*outs)
    return (outs[0], outs[1].reshape(224), outs[2].T, outs[3].T, outs[4].T)


def solution(mesh):
    both = P(("dp", "blk"), None)
    flat = P(("dp", "blk"))
    rows = P("blk", None)
    block = P("blk", "dp")
    return jax.shard_map(
        per_device,
        mesh=mesh,
        in_specs=(both, both, flat, flat, rows, rows, rows),
        out_specs=(both, flat, block, block, block),
        check_vma=False,
    )
```
